32 devices in a mesh: blk: 16 (over z, x, core), dim: 2 (over y).
Axes of the slice: x: 2, y: 2, z: 4, core: 2. Of those that a mesh axis runs over, the one named last changes fastest.
Arguments:
- points: bfloat16 [16384, 1024], P('blk', 'dim'), may hold values from -6 to 6
- owner: int32 [16384, 1], P('blk'), may hold values from 0 to 15; in each aligned block of 1024 rows (0 to 1023, 1024 to 2047, ...) at most 128 rows name the same one
- member: int32 [16384], P('blk'), may hold values from 0 to 8191
- centroids: bfloat16 [131072, 1024], P('blk', 'dim'), may hold values from -3 to 3
Outputs:
- new_centroids: bfloat16 [131072, 1024], P('blk', 'dim')
- nearest: float32 [16384], P('blk')
The draws below stay inside these ranges and needn't reach their ends.
Inputs may be any that keep to these rules, and one draw needn't show every extreme that they name: In the rows of one index of blk, no owner value occurs more than 128 times, and some value occurs exactly 128 times.
All inputs are finite; a program needn't handle non-finite values.
Results may differ from the reference program's by a relative error of at most 0.0004.
Values may be sent and summed in bfloat16 or wider, within the bound.
A program may use at most 128 MiB of HBM per device.

```python
import math
import jax
import jax.numpy as jnp
import numpy as np
from jax import lax

D = 1024
KC_DEV = 8192
PTS_DEV = 1024
CYCLE = 2
LISTS = 131072
POINTS = 16384
N_BLK = 16


def set_ends(array, stream_key, low, top_value):
    spot = [jax.random.randint(jax.random.fold_in(stream_key, axis), (), 0, length) for axis, length in enumerate(array.shape)]
    main_axis = array.shape.index(max(array.shape))
    neighbour = spot[:main_axis] + [(spot[main_axis] + 1) % array.shape[main_axis]] + spot[main_axis + 1:]
    return array.at[tuple(spot)].set(low).at[tuple(neighbour)].set(top_value)


def level_of(key, dims, shards, low, high):
    loudness = 1.0
    for position, parts in shards:
        heights = jax.random.uniform(jax.random.fold_in(jax.random.fold_in(key, 6), position), (parts,), jnp.float32, low / len(shards), high / len(shards))
        loudness = loudness * jnp.repeat(jnp.exp(heights), dims[position] // parts).reshape((-1,) + (1,) * (len(dims) - 1 - position))
    return loudness


def shared_out(stream_key, own, number, rows, amount, top, bound, lean):
    order = jax.random.permutation(stream_key, amount)
    packed, common = shares(amount, rows * top, bound, lean, True), shares(amount, rows * top, bound, lean, False)
    places = jnp.arange(amount)

    def named(sizes, rotation):
        used = int((sizes > 0).sum())
        fixed = max(1, used // 4)
        passed = fixed + (places - fixed + rotation * (used - fixed)) % max(1, amount - fixed)
        return jnp.zeros((amount,), jnp.int32).at[order[jnp.where(places < fixed, places, passed)]].set(jnp.asarray(sizes, jnp.int32))

    sizes = jnp.where(number % 4 == 0, named(packed, number // 4), named(common, number - number // 4 - 1))
    mixed = jax.random.permutation(jax.random.fold_in(own, 3), amount)
    giver, receiver = mixed[0:amount // 2 * 2:2], mixed[1:amount // 2 * 2:2]
    slack = jnp.minimum(sizes[giver] - 1, bound - sizes[receiver]) // 2
    slack = jnp.where((giver == order[0]) | (receiver == order[0]) | (sizes[receiver] == 0), 0, jnp.maximum(slack, 0))
    passed = jax.random.randint(jax.random.fold_in(own, 4), (amount // 2,), 0, 1 << 20) % (slack + 1)
    sizes = sizes.at[giver].add(-passed).at[receiver].add(passed)
    labels = jnp.searchsorted(jnp.cumsum(sizes), jnp.arange(rows * top), side="right").astype(jnp.int32)
    listing = labels.reshape(top, rows).T
    listing = listing[jax.random.permutation(jax.random.fold_in(own, 1), rows)]
    rotation = jax.random.randint(jax.random.fold_in(own, 2), (rows, 1), 0, top)
    return jnp.take_along_axis(listing, (jnp.arange(top)[None, :] + rotation) % top, axis=1)


def shares(amount, total, bound, skew, full):
    portions = [(1 << 20) // math.isqrt(rank ** skew) + 1 for rank in range(1, amount + 1)]
    largest = bound if full else min(bound, max(-(-total // amount), total * portions[0] // sum(portions)))
    least = 1 if total - largest >= amount - 1 else 0
    holding, rest = [largest] + [least] * (amount - 1), total - largest - least * (amount - 1)
    while rest > 0:
        candidates = [i for i in range(1, amount) if holding[i] < largest] or [i for i in range(1, amount) if holding[i] < bound]
        pool, budget = sum([portions[i] for i in candidates]), rest
        for i in candidates:
            addition = min(bound - holding[i], max(1, budget * portions[i] // pool), rest)
            holding[i] = holding[i] + addition
            rest = rest - addition
    return np.array(holding)


def centred(rng, shape, spread, most, shards=(), kind=jnp.bfloat16):
    array = spread * jax.random.normal(rng, shape, jnp.float32)
    if shards:
        array = array * level_of(rng, shape, shards, -0.22, 0.18)
    return jnp.clip(array, -most, most).astype(kind)


def setup_inputs(seed: int = 0) -> dict:
    streams_of = jax.random.split(jax.random.key(seed), 5)
    points = centred(streams_of[0], (POINTS, D), 1.0, 6.0, ((0, 16), (1, 2)))
    owner_keys = jax.random.split(jax.random.fold_in(streams_of[1], 1), POINTS // PTS_DEV)
    owner_turns = jax.random.permutation(jax.random.fold_in(streams_of[1], 3), POINTS // PTS_DEV)
    owner = jax.vmap(lambda own, number: shared_out(jax.random.fold_in(streams_of[1], 2), own, number, PTS_DEV, N_BLK, 1, 2 * PTS_DEV // N_BLK, 2))(owner_keys, owner_turns).reshape((POINTS, 1))
    member = set_ends(jax.random.randint(streams_of[2], (POINTS,), 0, KC_DEV), jax.random.fold_in(streams_of[2], 1), 0, KC_DEV - 1).astype(jnp.int32)
    centroids = centred(streams_of[3], (LISTS, D), 0.5, 3.0, ((0, 16), (1, 2)))
    return dict(points=points, owner=owner, member=member, centroids=centroids)


def reference(points, owner, member, centroids):
    owners = owner[:, 0]
    point_floats = points.astype(jnp.float32)

    def block_update(index):
        target = jnp.where(owners == index, member, KC_DEV)
        sums = jnp.zeros((KC_DEV, D), jnp.float32).at[target].add(point_floats, mode="drop")
        counts = jnp.zeros((KC_DEV,), jnp.float32).at[target].add(jnp.ones(target.shape, jnp.float32), mode="drop")
        olds = lax.dynamic_slice_in_dim(centroids, (index * KC_DEV).astype(jnp.int32), KC_DEV, 0)
        return ((sums + olds.astype(jnp.float32)) / (counts[:, None] + 1.0)).astype(jnp.bfloat16)

    updated = lax.map(block_update, jnp.arange(N_BLK, dtype=jnp.int32))

    def block_nearest(index):
        rows = lax.dynamic_slice_in_dim(points, (index * PTS_DEV).astype(jnp.int32), PTS_DEV, 0)
        row_floats = rows.astype(jnp.float32)
        squares = jnp.sum(row_floats * row_floats, axis=1)
        best = jnp.full((PTS_DEV,), jnp.inf, jnp.float32)
        for section in range(CYCLE + 1):
            source = ((index - section) % N_BLK).astype(jnp.int32)
            candidate = updated[source]
            cand_floats = candidate.astype(jnp.float32)
            cand_squares = jnp.sum(cand_floats * cand_floats, axis=1)
            inner = lax.dot_general(rows, candidate, (((1,), (1,)), ((), ())), preferred_element_type=jnp.float32)
            distance = (squares[:, None] + cand_squares[None, :] - 2.0 * inner) / D
            best = jnp.minimum(best, jnp.min(distance, axis=1))
        return best

    nearest = lax.map(block_nearest, jnp.arange(N_BLK, dtype=jnp.int32))
    return updated.reshape(LISTS, D), nearest.reshape(POINTS)
```

```python
import functools

import jax
import jax.numpy as jnp
from jax import lax
from jax.experimental import pallas as pl
from jax.experimental.pallas import tpu as pltpu
from jax.sharding import PartitionSpec as P

CYCLE = 2
LANES = 128
MESH = pl.DeviceIdType.MESH
NT = (((1,), (1,)), ((), ()))
F32, BF16, I32 = jnp.float32, jnp.bfloat16, jnp.int32


def kernel(
    n, slots, tile,
    owner_ref, member_ref, points_hbm, cent_hbm,
    new_hbm, near_ref,
    pts, cent, cand, send, recv, isend, irecv, idx_row, slot_row, mins, got, squares,
    load_sem, row_send, row_recv, ind_send, ind_recv, pt_send, pt_recv,
    ring_send, ring_recv, chunk_send, chunk_recv, out_sem, min_send, min_recv,
):
    rows, half = points_hbm.shape
    lists = cent_hbm.shape[0]
    keep = lists // 2
    chunks = keep // tile
    total = n * slots
    share = LANES // slots
    me, side = lax.axis_index("blk"), lax.axis_index("dim")
    other = 1 - side

    load_points = pltpu.make_async_copy(points_hbm, pts.at[0, :, pl.ds(0, half)], load_sem.at[0])
    load_points.start()
    load_cent = pltpu.make_async_copy(cent_hbm, cent, load_sem.at[1])
    load_cent.start()

    barrier = pltpu.get_barrier_semaphore()

    def greet(d, carry):
        pl.semaphore_signal(
            barrier, inc=1, device_id=(lax.rem(me + d, n), side), device_id_type=MESH)
        return carry

    lax.fori_loop(1, n, greet, 0)
    for s in range(-CYCLE, CYCLE + 1):
        pl.semaphore_signal(
            barrier, inc=1, device_id=(lax.rem(me + s + n, n), other), device_id_type=MESH)

    owner = owner_ref[...]
    owned = lax.broadcasted_iota(I32, (n, rows), 0) == owner
    before = lax.broadcasted_iota(I32, (rows, rows), 0) < lax.broadcasted_iota(I32, (rows, rows), 1)
    earlier = jnp.dot(
        owned.astype(F32).astype(BF16), before.astype(F32).astype(BF16), preferred_element_type=F32)
    rank = jnp.sum(jnp.where(owned, earlier, 0.0), axis=0, keepdims=True).astype(I32)
    slot_row[...] = jnp.broadcast_to(owner * slots + rank, slot_row.shape)

    code = member_ref[...] + 1
    shift = slots * lax.rem(me, share)
    lane_of = (lax.broadcasted_iota(I32, (LANES, rows), 0) == rank + shift).astype(F32).astype(BF16)
    high = jnp.where(owned, (code >> 7).astype(F32), 0.0).astype(BF16)
    low = jnp.where(owned, (code & 127).astype(F32), 0.0).astype(BF16)
    codes = 128.0 * lax.dot_general(high, lane_of, NT, preferred_element_type=F32)
    codes = codes + lax.dot_general(low, lane_of, NT, preferred_element_type=F32)
    codes = codes.astype(I32)
    for j in range(n):
        isend[j] = jnp.broadcast_to(codes[j:j + 1, :], isend.shape[1:])

    load_points.wait()
    pl.semaphore_wait(barrier, n - 1 + 2 * CYCLE + 1)

    own_pts = pts.at[0, :, pl.ds(0, half)]
    point_copy = pltpu.make_async_remote_copy(
        src_ref=own_pts, dst_ref=pts.at[0, :, pl.ds(half, half)],
        send_sem=pt_send, recv_sem=pt_recv, device_id=(me, other), device_id_type=MESH)
    point_copy.start()

    def pack(j):
        base = pl.multiple_of(j * slots, slots)
        place = lax.broadcasted_iota(I32, (slots, rows), 0) + base
        pick = (place == slot_row[0:1, :]).astype(F32).astype(BF16)
        packed = jnp.dot(pick, pts[0, :, 0:half], preferred_element_type=F32).astype(BF16)
        return base, packed

    def copies(d):
        j = lax.rem(me + d, n)
        there = pl.ds(pl.multiple_of(me * slots, slots), slots)
        row_copy = pltpu.make_async_remote_copy(
            src_ref=send.at[pl.ds(pl.multiple_of(j * slots, slots), slots)], dst_ref=recv.at[there],
            send_sem=row_send.at[d], recv_sem=row_recv.at[d],
            device_id=(j, side), device_id_type=MESH)
        ind_copy = pltpu.make_async_remote_copy(
            src_ref=isend.at[j], dst_ref=irecv.at[me],
            send_sem=ind_send.at[d], recv_sem=ind_recv.at[d],
            device_id=(j, side), device_id_type=MESH)
        return row_copy, ind_copy

    def dispatch(i, carry):
        d = 1 + lax.rem(i + n // 4, n - 1)
        base, packed = pack(lax.rem(me + d, n))
        send[pl.ds(base, slots), :] = packed
        row_copy, ind_copy = copies(d)
        ind_copy.start()
        row_copy.start()
        return carry

    lax.fori_loop(0, n - 1, dispatch, 0)
    base, packed = pack(me)
    recv[pl.ds(base, slots), :] = packed
    irecv[me] = isend[me]

    point_copy.wait()
    ones = jnp.ones((8, 2 * half), BF16)
    block = min(256, rows)
    for r in range(rows // block):
        p = pts[0, r * block:(r + 1) * block, :].astype(F32)
        sq = p * p
        top = sq.astype(BF16)
        rest = (sq - top.astype(F32)).astype(BF16)
        squares[:, r * block:(r + 1) * block] = lax.dot_general(
            ones, top, NT, preferred_element_type=F32
        ) + lax.dot_general(ones, rest, NT, preferred_element_type=F32)
    mins[...] = jnp.full(mins.shape, jnp.inf, F32)
    load_cent.wait()

    def arrive(d, carry):
        row_copy, ind_copy = copies(d)
        ind_copy.wait()
        row_copy.wait()
        return carry

    lax.fori_loop(1, n, arrive, 0)
    for g in range(total // LANES):
        line = irecv[g * share]
        for i in range(1, share):
            line = line + irecv[g * share + i]
        idx_row[:, g * LANES:(g + 1) * LANES] = line

    previous = lax.rem(me + n - 1, n)

    def ring(s):
        return pltpu.make_async_remote_copy(
            src_ref=pts.at[s - 1], dst_ref=pts.at[s],
            send_sem=ring_send.at[s - 1], recv_sem=ring_recv.at[s - 1],
            device_id=(previous, side), device_id_type=MESH)

    ring(1).start()

    def updated(first):
        number = lax.broadcasted_iota(I32, (tile, total), 0) + (first + 1)
        hot = (number == idx_row[0:1, :]).astype(F32)
        count = jnp.sum(hot, axis=1, keepdims=True)
        sums = jnp.dot(hot.astype(BF16), recv[...], preferred_element_type=F32)
        old = cent[pl.ds(first, tile), :].astype(F32)
        return ((sums + old) * (1.0 / (count + 1.0))).astype(BF16)

    def start_of(c, whose):
        return pl.multiple_of(whose * keep + c * tile, tile)

    def chunk_copy(c):
        return pltpu.make_async_remote_copy(
            src_ref=cent.at[pl.ds(start_of(c, other), tile)],
            dst_ref=cand.at[pl.ds(pl.multiple_of(c * tile, tile), tile), pl.ds(half, half)],
            send_sem=chunk_send.at[c], recv_sem=chunk_recv.at[c],
            device_id=(me, other), device_id_type=MESH)

    def sent_out(c):
        place = pl.ds(start_of(c, other), tile)
        return pltpu.make_async_copy(cent.at[place], new_hbm.at[place], out_sem.at[0, c])

    def kept_out(c):
        here = pl.ds(pl.multiple_of(c * tile, tile), tile)
        return pltpu.make_async_copy(
            cand.at[here, pl.ds(0, half)], new_hbm.at[pl.ds(start_of(c, side), tile)],
            out_sem.at[1, c])

    def give(c, carry):
        first = start_of(c, other)
        cent[pl.ds(first, tile), :] = updated(first)
        chunk_copy(c).start()
        sent_out(c).start()
        return carry

    lax.fori_loop(0, chunks, give, 0)
    for s in range(1, CYCLE):
        ring(s).wait_recv()
        ring(s + 1).start()

    def hold(c, carry):
        here = pl.ds(pl.multiple_of(c * tile, tile), tile)
        cand[here, 0:half] = updated(start_of(c, side))
        kept_out(c).start()
        return carry

    lax.fori_loop(0, chunks, hold, 0)
    ring(CYCLE).wait_recv()

    def search(c, carry):
        chunk_copy(c).wait_recv()
        block_c = cand[pl.ds(pl.multiple_of(c * tile, tile), tile), :]
        wide = block_c.astype(F32)
        half_square = 0.5 * jnp.sum(wide * wide, axis=1, keepdims=True)
        for s in range(CYCLE + 1):
            inner = lax.dot_general(block_c, pts[s], NT, preferred_element_type=F32)
            value = (half_square - inner).reshape(tile // 8, 8, rows)
            mins[s] = jnp.minimum(mins[s], jnp.min(value, axis=0))
        return carry

    lax.fori_loop(0, chunks, search, 0)

    back = []
    for s in range(CYCLE + 1):
        for way in range(2):
            if s == 0 and way == 0:
                continue
            back.append(pltpu.make_async_remote_copy(
                src_ref=mins.at[s], dst_ref=got.at[way, s],
                send_sem=min_send.at[way, s], recv_sem=min_recv.at[way, s],
                device_id=(lax.rem(me + s, n), other if way else side), device_id_type=MESH))
    for copy in back:
        copy.start()

    def finish(c, carry):
        chunk_copy(c).wait_send()
        sent_out(c).wait()
        kept_out(c).wait()
        return carry

    lax.fori_loop(0, chunks, finish, 0)
    for s in range(1, CYCLE + 1):
        ring(s).wait_send()
    for copy in back:
        copy.wait()
    best = mins[0]
    for s in range(CYCLE + 1):
        for way in range(2):
            if s or way:
                best = jnp.minimum(best, got[way, s])
    least = jnp.min(best, axis=0, keepdims=True)
    near_ref[...] = (squares[0:1, :] + 2.0 * least) / (2 * half)


def shards(points, owner, member, centroids):
    n = lax.axis_size("blk")
    rows, half = points.shape
    lists = centroids.shape[0]
    slots = 2 * rows // n
    tile = min(256, lists // 4)
    chunks = lists // 2 // tile
    total = n * slots
    anywhere, vmem = pl.BlockSpec(memory_space=pl.ANY), pl.BlockSpec(memory_space=pltpu.VMEM)
    dma = pltpu.SemaphoreType.DMA
    new, near = pl.pallas_call(
        functools.partial(kernel, n, slots, tile),
        out_shape=(
            jax.ShapeDtypeStruct(centroids.shape, BF16),
            jax.ShapeDtypeStruct((1, rows), F32),
        ),
        in_specs=[vmem, vmem, anywhere, anywhere],
        out_specs=(anywhere, vmem),
        scratch_shapes=[
            pltpu.VMEM((CYCLE + 1, rows, 2 * half), BF16),
            pltpu.VMEM((lists, half), BF16),
            pltpu.VMEM((lists // 2, 2 * half), BF16),
            pltpu.VMEM((total, half), BF16),
            pltpu.VMEM((total, half), BF16),
            pltpu.VMEM((n, 8, LANES), I32),
            pltpu.VMEM((n, 8, LANES), I32),
            pltpu.VMEM((8, total), I32),
            pltpu.VMEM((8, rows), I32),
            pltpu.VMEM((CYCLE + 1, 8, rows), F32),
            pltpu.VMEM((2, CYCLE + 1, 8, rows), F32),
            pltpu.VMEM((8, rows), F32),
            dma((2,)), dma((n,)), dma((n,)), dma((n,)), dma((n,)), dma, dma,
            dma((CYCLE,)), dma((CYCLE,)), dma((chunks,)), dma((chunks,)), dma((2, chunks)),
            dma((2, CYCLE + 1)), dma((2, CYCLE + 1)),
        ],
        compiler_params=pltpu.CompilerParams(
            collective_id=0, has_side_effects=True, vmem_limit_bytes=56 * 1024 * 1024),
    )(owner.reshape(1, rows), member.reshape(1, rows), points, centroids)
    return new, near.reshape(rows)


def solution(mesh):
    in_specs = (P("blk", "dim"), P("blk", None), P("blk"), P("blk", "dim"))
    out_specs = (P("blk", "dim"), P("blk"))
    return jax.shard_map(shards, mesh=mesh, in_specs=in_specs, out_specs=out_specs, check_vma=False)
```

```python
import functools

import jax
import jax.numpy as jnp
from jax import lax
from jax.experimental import pallas as pl
from jax.experimental.pallas import tpu as pltpu
from jax.sharding import PartitionSpec as P

CYCLE = 2
LANES = 128
MESH = pl.DeviceIdType.MESH
NT = (((1,), (1,)), ((), ()))
F32, BF16, I32 = jnp.float32, jnp.bfloat16, jnp.int32


def kernel(
    n, slots, units,
    owner_ref, member_ref, points_hbm, cent_hbm,
    new_hbm, near_ref,
    pts, cent, cand, send, recv, isend, irecv, idx_row, slot_row, mins, got, squares,
    load_sem, row_send, row_recv, ind_send, ind_recv, pt_send, pt_recv,
    ring_send, ring_recv, chunk_send, chunk_recv, out_sem, min_send, min_recv,
):
    rows, half = points_hbm.shape
    lists = cent_hbm.shape[0]
    keep = lists // 2
    unit = keep // units
    piece = unit // 2
    total = n * slots
    share = LANES // slots
    me, side = lax.axis_index("blk"), lax.axis_index("dim")
    other = 1 - side

    load_points = pltpu.make_async_copy(points_hbm, pts.at[0, :, pl.ds(0, half)], load_sem.at[0])
    load_points.start()
    load_cent = pltpu.make_async_copy(cent_hbm, cent, load_sem.at[1])
    load_cent.start()

    barrier = pltpu.get_barrier_semaphore()

    def greet(d, carry):
        pl.semaphore_signal(
            barrier, inc=1, device_id=(lax.rem(me + d, n), side), device_id_type=MESH)
        return carry

    lax.fori_loop(1, n, greet, 0)
    for s in range(-CYCLE, CYCLE + 1):
        pl.semaphore_signal(
            barrier, inc=1, device_id=(lax.rem(me + s + n, n), other), device_id_type=MESH)

    owner = owner_ref[...]
    owned = lax.broadcasted_iota(I32, (n, rows), 0) == owner
    before = lax.broadcasted_iota(I32, (rows, rows), 0) < lax.broadcasted_iota(I32, (rows, rows), 1)
    earlier = jnp.dot(
        owned.astype(F32).astype(BF16), before.astype(F32).astype(BF16), preferred_element_type=F32)
    rank = jnp.sum(jnp.where(owned, earlier, 0.0), axis=0, keepdims=True).astype(I32)
    slot_row[...] = jnp.broadcast_to(owner * slots + rank, slot_row.shape)

    code = member_ref[...] + 1
    shift = slots * lax.rem(me, share)
    lane_of = (lax.broadcasted_iota(I32, (LANES, rows), 0) == rank + shift).astype(F32).astype(BF16)
    high = jnp.where(owned, (code >> 7).astype(F32), 0.0).astype(BF16)
    low = jnp.where(owned, (code & 127).astype(F32), 0.0).astype(BF16)
    codes = 128.0 * lax.dot_general(high, lane_of, NT, preferred_element_type=F32)
    codes = codes + lax.dot_general(low, lane_of, NT, preferred_element_type=F32)
    codes = codes.astype(I32)
    for j in range(n):
        isend[j] = jnp.broadcast_to(codes[j:j + 1, :], isend.shape[1:])

    load_points.wait()
    pl.semaphore_wait(barrier, n - 1 + 2 * CYCLE + 1)

    own_pts = pts.at[0, :, pl.ds(0, half)]
    point_copy = pltpu.make_async_remote_copy(
        src_ref=own_pts, dst_ref=pts.at[0, :, pl.ds(half, half)],
        send_sem=pt_send, recv_sem=pt_recv, device_id=(me, other), device_id_type=MESH)
    point_copy.start()

    def pack(j):
        base = pl.multiple_of(j * slots, slots)
        place = lax.broadcasted_iota(I32, (slots, rows), 0) + base
        pick = (place == slot_row[0:1, :]).astype(F32).astype(BF16)
        packed = jnp.dot(pick, pts[0, :, 0:half], preferred_element_type=F32).astype(BF16)
        return base, packed

    def copies(d):
        j = lax.rem(me + d, n)
        there = pl.ds(pl.multiple_of(me * slots, slots), slots)
        row_copy = pltpu.make_async_remote_copy(
            src_ref=send.at[pl.ds(pl.multiple_of(j * slots, slots), slots)], dst_ref=recv.at[there],
            send_sem=row_send.at[d], recv_sem=row_recv.at[d],
            device_id=(j, side), device_id_type=MESH)
        ind_copy = pltpu.make_async_remote_copy(
            src_ref=isend.at[j], dst_ref=irecv.at[me],
            send_sem=ind_send.at[d], recv_sem=ind_recv.at[d],
            device_id=(j, side), device_id_type=MESH)
        return row_copy, ind_copy

    def dispatch(i, carry):
        d = 1 + lax.rem(i + n // 4, n - 1)
        base, packed = pack(lax.rem(me + d, n))
        send[pl.ds(base, slots), :] = packed
        row_copy, ind_copy = copies(d)
        ind_copy.start()
        row_copy.start()
        return carry

    lax.fori_loop(0, n - 1, dispatch, 0)
    base, packed = pack(me)
    recv[pl.ds(base, slots), :] = packed
    irecv[me] = isend[me]

    point_copy.wait()
    odd = lax.rem(me, 2) == 1

    def ring(source, back, slot, sem):
        return pltpu.make_async_remote_copy(
            src_ref=pts.at[source], dst_ref=pts.at[slot],
            send_sem=ring_send.at[sem], recv_sem=ring_recv.at[slot - 1],
            device_id=(lax.rem(me + n - back, n), side), device_id_type=MESH)

    to_one, to_two, handed = ring(0, 1, 1, 0), ring(0, 2, 2, 1), ring(1, 1, 2, 2)

    @pl.when(odd)
    def _():
        to_one.start()

    ones = jnp.ones((8, 2 * half), BF16)
    block = min(256, rows)
    for r in range(rows // block):
        p = pts[0, r * block:(r + 1) * block, :].astype(F32)
        sq = p * p
        top = sq.astype(BF16)
        rest = (sq - top.astype(F32)).astype(BF16)
        squares[:, r * block:(r + 1) * block] = lax.dot_general(
            ones, top, NT, preferred_element_type=F32
        ) + lax.dot_general(ones, rest, NT, preferred_element_type=F32)
    mins[...] = jnp.full(mins.shape, jnp.inf, F32)
    load_cent.wait()

    def arrive(d, carry):
        row_copy, ind_copy = copies(d)
        ind_copy.wait()
        row_copy.wait()
        return carry

    lax.fori_loop(1, n, arrive, 0)
    for g in range(total // LANES):
        line = irecv[g * share]
        for i in range(1, share):
            line = line + irecv[g * share + i]
        idx_row[:, g * LANES:(g + 1) * LANES] = line

    @pl.when(odd)
    def _():
        to_two.start()

    @pl.when(jnp.logical_not(odd))
    def _():
        to_one.start()

    def updated(first, size):
        wanted = idx_row[0:1, :] - (first + 1)
        hot = (lax.broadcasted_iota(I32, (size, total), 0) == wanted).astype(F32)
        count = jnp.sum(hot, axis=1, keepdims=True)
        sums = jnp.dot(hot.astype(BF16), recv[...], preferred_element_type=F32)
        old = cent[pl.ds(first, size), :].astype(F32)
        return ((sums + old) * (1.0 / (count + 1.0))).astype(BF16)

    def at(start, size):
        return pl.ds(pl.multiple_of(start, piece), size)

    def chunk_copy(c, start, size):
        return pltpu.make_async_remote_copy(
            src_ref=cent.at[at(other * keep + start, size)],
            dst_ref=cand.at[at(start, size), pl.ds(half, half)],
            send_sem=chunk_send.at[c], recv_sem=chunk_recv.at[c],
            device_id=(me, other), device_id_type=MESH)

    def sent_out(c, start, size):
        place = at(other * keep + start, size)
        return pltpu.make_async_copy(cent.at[place], new_hbm.at[place], out_sem.at[0, c])

    def kept_out(u):
        return pltpu.make_async_copy(
            cand.at[at(u * unit, unit), pl.ds(0, half)],
            new_hbm.at[at(side * keep + u * unit, unit)], out_sem.at[1, u])

    def give(c, start, size):
        first = pl.multiple_of(other * keep + start, piece)
        cent[pl.ds(first, size), :] = updated(first, size)
        chunk_copy(c, start, size).start()
        sent_out(c, start, size).start()

    last = (units - 1) * unit
    ends = [(0, 0), (1, piece), (units, last), (units + 1, last + piece)]

    def loop(low, high, body):
        def step(u, carry):
            body(u)
            return carry
        lax.fori_loop(low, high, step, 0)

    def hold(u):
        cand[at(u * unit, unit), 0:half] = updated(pl.multiple_of(side * keep + u * unit, unit), unit)
        kept_out(u).start()

    for c, start in ends[:2]:
        give(c, start, piece)
    loop(1, units - 1, lambda u: give(u + 1, u * unit, unit))
    for c, start in ends[2:]:
        give(c, start, piece)
    loop(0, units, hold)

    def search(start, size, sections):
        block_c = cand[at(start, size), :]
        wide = block_c.astype(F32)
        half_square = 0.5 * jnp.sum(wide * wide, axis=1, keepdims=True)
        for s in sections:
            inner = lax.dot_general(block_c, pts[s], NT, preferred_element_type=F32)
            value = (half_square - inner).reshape(size // 8, 8, rows)
            mins[s] = jnp.minimum(mins[s], jnp.min(value, axis=0))

    def arrived(u, sections):
        chunk_copy(u + 1, u * unit, unit).wait_recv()
        search(u * unit, unit, sections)

    for c, start in ends[:2]:
        chunk_copy(c, start, piece).wait_recv()
    search(0, unit, (0,))
    loop(1, units // 2, lambda u: arrived(u, (0,)))
    to_one.wait_recv()

    @pl.when(odd)
    def _():
        handed.start()

    loop(0, units // 2, lambda u: search(u * unit, unit, (1,)))
    loop(units // 2, units - 2, lambda u: arrived(u, (0, 1)))
    to_two.wait_recv()
    loop(0, units - 2, lambda u: search(u * unit, unit, (2,)))
    arrived(units - 2, range(CYCLE + 1))
    for c, start in ends[2:]:
        chunk_copy(c, start, piece).wait_recv()
        search(start, piece, range(CYCLE + 1))

    back = []
    for s in range(CYCLE + 1):
        for way in range(2):
            if s == 0 and way == 0:
                continue
            back.append(pltpu.make_async_remote_copy(
                src_ref=mins.at[s], dst_ref=got.at[way, s],
                send_sem=min_send.at[way, s], recv_sem=min_recv.at[way, s],
                device_id=(lax.rem(me + s, n), other if way else side), device_id_type=MESH))
    for copy in back:
        copy.start()

    def gone(c, start, size):
        chunk_copy(c, start, size).wait_send()
        sent_out(c, start, size).wait()

    for c, start in ends:
        gone(c, start, piece)
    loop(1, units - 1, lambda u: gone(u + 1, u * unit, unit))
    loop(0, units, lambda u: kept_out(u).wait())
    to_one.wait_send()

    @pl.when(odd)
    def _():
        to_two.wait_send()
        handed.wait_send()

    for copy in back:
        copy.wait()
    best = mins[0]
    for s in range(CYCLE + 1):
        for way in range(2):
            if s or way:
                best = jnp.minimum(best, got[way, s])
    least = jnp.min(best, axis=0, keepdims=True)
    near_ref[...] = (squares[0:1, :] + 2.0 * least) / (2 * half)


def shards(points, owner, member, centroids):
    n = lax.axis_size("blk")
    rows, half = points.shape
    lists = centroids.shape[0]
    slots = 2 * rows // n
    units = 8
    chunks = units + 2
    total = n * slots
    anywhere, vmem = pl.BlockSpec(memory_space=pl.ANY), pl.BlockSpec(memory_space=pltpu.VMEM)
    dma = pltpu.SemaphoreType.DMA
    new, near = pl.pallas_call(
        functools.partial(kernel, n, slots, units),
        out_shape=(
            jax.ShapeDtypeStruct(centroids.shape, BF16),
            jax.ShapeDtypeStruct((1, rows), F32),
        ),
        in_specs=[vmem, vmem, anywhere, anywhere],
        out_specs=(anywhere, vmem),
        scratch_shapes=[
            pltpu.VMEM((CYCLE + 1, rows, 2 * half), BF16),
            pltpu.VMEM((lists, half), BF16),
            pltpu.VMEM((lists // 2, 2 * half), BF16),
            pltpu.VMEM((total, half), BF16),
            pltpu.VMEM((total, half), BF16),
            pltpu.VMEM((n, 8, LANES), I32),
            pltpu.VMEM((n, 8, LANES), I32),
            pltpu.VMEM((8, total), I32),
            pltpu.VMEM((8, rows), I32),
            pltpu.VMEM((CYCLE + 1, 8, rows), F32),
            pltpu.VMEM((2, CYCLE + 1, 8, rows), F32),
            pltpu.VMEM((8, rows), F32),
            dma((2,)), dma((n,)), dma((n,)), dma((n,)), dma((n,)), dma, dma,
            dma((CYCLE + 1,)), dma((CYCLE,)), dma((chunks,)), dma((chunks,)), dma((2, chunks)),
            dma((2, CYCLE + 1)), dma((2, CYCLE + 1)),
        ],
        compiler_params=pltpu.CompilerParams(
            collective_id=0, has_side_effects=True, vmem_limit_bytes=56 * 1024 * 1024),
    )(owner.reshape(1, rows), member.reshape(1, rows), points, centroids)
    return new, near.reshape(rows)


def solution(mesh):
    in_specs = (P("blk", "dim"), P("blk", None), P("blk"), P("blk", "dim"))
    out_specs = (P("blk", "dim"), P("blk"))
    return jax.shard_map(shards, mesh=mesh, in_specs=in_specs, out_specs=out_specs, check_vma=False)
```

```python
import functools

import jax
import jax.numpy as jnp
from jax import lax
from jax.experimental import pallas as pl
from jax.experimental.pallas import tpu as pltpu
from jax.sharding import PartitionSpec as P

CYCLE = 2
LANES = 128
MESH = pl.DeviceIdType.MESH
NT = (((1,), (1,)), ((), ()))
F32, BF16, I32 = jnp.float32, jnp.bfloat16, jnp.int32


def kernel(
    n, slots, units,
    owner_ref, member_ref, points_hbm, cent_hbm,
    new_hbm, near_ref,
    pts, cent, cand, send, recv, isend, irecv, idx_row, slot_row, mins, got, squares,
    load_sem, row_send, row_recv, ind_send, ind_recv, pt_send, pt_recv,
    ring_send, ring_recv, chunk_send, chunk_recv, out_sem, min_send, min_recv,
):
    rows, half = points_hbm.shape
    lists = cent_hbm.shape[0]
    keep = lists // 2
    unit = keep // units
    piece = unit // 2
    total = n * slots
    share = LANES // slots
    me, side = lax.axis_index("blk"), lax.axis_index("dim")
    other = 1 - side

    load_points = pltpu.make_async_copy(points_hbm, pts.at[0, :, pl.ds(0, half)], load_sem.at[0])
    load_points.start()
    load_cent = pltpu.make_async_copy(cent_hbm, cent, load_sem.at[1])
    load_cent.start()

    barrier = pltpu.get_barrier_semaphore()

    def greet(d, carry):
        pl.semaphore_signal(
            barrier, inc=1, device_id=(lax.rem(me + d, n), side), device_id_type=MESH)
        return carry

    lax.fori_loop(1, n, greet, 0)
    for s in range(-CYCLE, CYCLE + 1):
        pl.semaphore_signal(
            barrier, inc=1, device_id=(lax.rem(me + s + n, n), other), device_id_type=MESH)

    owner = owner_ref[...]
    owned = lax.broadcasted_iota(I32, (n, rows), 0) == owner
    before = lax.broadcasted_iota(I32, (rows, rows), 0) < lax.broadcasted_iota(I32, (rows, rows), 1)
    earlier = jnp.dot(
        owned.astype(F32).astype(BF16), before.astype(F32).astype(BF16), preferred_element_type=F32)
    rank = jnp.sum(jnp.where(owned, earlier, 0.0), axis=0, keepdims=True).astype(I32)
    slot_row[...] = jnp.broadcast_to(owner * slots + rank, slot_row.shape)

    code = member_ref[...] + 1
    shift = slots * lax.rem(me, share)
    lane_of = (lax.broadcasted_iota(I32, (LANES, rows), 0) == rank + shift).astype(F32).astype(BF16)
    high = jnp.where(owned, (code >> 7).astype(F32), 0.0).astype(BF16)
    low = jnp.where(owned, (code & 127).astype(F32), 0.0).astype(BF16)
    codes = 128.0 * lax.dot_general(high, lane_of, NT, preferred_element_type=F32)
    codes = codes + lax.dot_general(low, lane_of, NT, preferred_element_type=F32)
    codes = codes.astype(I32)
    for j in range(n):
        isend[j] = jnp.broadcast_to(codes[j:j + 1, :], isend.shape[1:])

    load_points.wait()
    pl.semaphore_wait(barrier, n - 1 + 2 * CYCLE + 1)

    own_pts = pts.at[0, :, pl.ds(0, half)]
    point_copy = pltpu.make_async_remote_copy(
        src_ref=own_pts, dst_ref=pts.at[0, :, pl.ds(half, half)],
        send_sem=pt_send, recv_sem=pt_recv, device_id=(me, other), device_id_type=MESH)
    point_copy.start()

    def pack(j):
        base = pl.multiple_of(j * slots, slots)
        place = lax.broadcasted_iota(I32, (slots, rows), 0) + base
        pick = (place == slot_row[0:1, :]).astype(F32).astype(BF16)
        packed = jnp.dot(pick, pts[0, :, 0:half], preferred_element_type=F32).astype(BF16)
        return base, packed

    def copies(d):
        j = lax.rem(me + d, n)
        there = pl.ds(pl.multiple_of(me * slots, slots), slots)
        row_copy = pltpu.make_async_remote_copy(
            src_ref=send.at[pl.ds(pl.multiple_of(j * slots, slots), slots)], dst_ref=recv.at[there],
            send_sem=row_send.at[d], recv_sem=row_recv.at[d],
            device_id=(j, side), device_id_type=MESH)
        ind_copy = pltpu.make_async_remote_copy(
            src_ref=isend.at[j], dst_ref=irecv.at[me],
            send_sem=ind_send.at[d], recv_sem=ind_recv.at[d],
            device_id=(j, side), device_id_type=MESH)
        return row_copy, ind_copy

    def dispatch(i, carry):
        d = n // 2 + ((i + 1) // 2) * (1 - 2 * lax.rem(i, 2))
        base, packed = pack(lax.rem(me + d, n))
        send[pl.ds(base, slots), :] = packed
        row_copy, ind_copy = copies(d)
        ind_copy.start()
        row_copy.start()
        return carry

    lax.fori_loop(0, n - 1, dispatch, 0)
    base, packed = pack(me)
    recv[pl.ds(base, slots), :] = packed
    irecv[me] = isend[me]

    point_copy.wait()
    odd = lax.rem(me, 2) == 1

    def ring(source, back, slot, sem):
        return pltpu.make_async_remote_copy(
            src_ref=pts.at[source], dst_ref=pts.at[slot],
            send_sem=ring_send.at[sem], recv_sem=ring_recv.at[slot - 1],
            device_id=(lax.rem(me + n - back, n), side), device_id_type=MESH)

    to_one, to_two, handed = ring(0, 1, 1, 0), ring(0, 2, 2, 1), ring(1, 1, 2, 2)

    @pl.when(odd)
    def _():
        to_one.start()

    ones = jnp.ones((8, 2 * half), BF16)
    block = min(256, rows)
    for r in range(rows // block):
        p = pts[0, r * block:(r + 1) * block, :].astype(F32)
        sq = p * p
        top = sq.astype(BF16)
        rest = (sq - top.astype(F32)).astype(BF16)
        squares[:, r * block:(r + 1) * block] = lax.dot_general(
            ones, top, NT, preferred_element_type=F32
        ) + lax.dot_general(ones, rest, NT, preferred_element_type=F32)
    mins[...] = jnp.full(mins.shape, jnp.inf, F32)
    load_cent.wait()

    def arrive(d, carry):
        row_copy, ind_copy = copies(d)
        ind_copy.wait()
        row_copy.wait()
        return carry

    lax.fori_loop(1, n, arrive, 0)
    for g in range(total // LANES):
        line = irecv[g * share]
        for i in range(1, share):
            line = line + irecv[g * share + i]
        idx_row[:, g * LANES:(g + 1) * LANES] = line

    def updated(first, size):
        wanted = idx_row[0:1, :] - (first + 1)
        hot = (lax.broadcasted_iota(I32, (size, total), 0) == wanted).astype(F32)
        count = jnp.sum(hot, axis=1, keepdims=True)
        sums = jnp.dot(hot.astype(BF16), recv[...], preferred_element_type=F32)
        old = cent[pl.ds(first, size), :].astype(F32)
        return ((sums + old) * (1.0 / (count + 1.0))).astype(BF16)

    def at(start, size):
        return pl.ds(pl.multiple_of(start, piece), size)

    def chunk_copy(c, start, size):
        return pltpu.make_async_remote_copy(
            src_ref=cent.at[at(other * keep + start, size)],
            dst_ref=cand.at[at(start, size), pl.ds(half, half)],
            send_sem=chunk_send.at[c], recv_sem=chunk_recv.at[c],
            device_id=(me, other), device_id_type=MESH)

    def sent_out(c, start, size):
        place = at(other * keep + start, size)
        return pltpu.make_async_copy(cent.at[place], new_hbm.at[place], out_sem.at[0, c])

    def kept_out(u):
        return pltpu.make_async_copy(
            cand.at[at(u * unit, unit), pl.ds(0, half)],
            new_hbm.at[at(side * keep + u * unit, unit)], out_sem.at[1, u])

    def give(c, start, size):
        first = pl.multiple_of(other * keep + start, piece)
        cent[pl.ds(first, size), :] = updated(first, size)
        chunk_copy(c, start, size).start()
        sent_out(c, start, size).start()

    last = (units - 1) * unit
    ends = [(0, 0), (1, piece), (units, last), (units + 1, last + piece)]

    def loop(low, high, body):
        def step(u, carry):
            body(u)
            return carry
        lax.fori_loop(low, high, step, 0)

    def hold(u):
        cand[at(u * unit, unit), 0:half] = updated(pl.multiple_of(side * keep + u * unit, unit), unit)
        kept_out(u).start()

    for c, start in ends[:2]:
        give(c, start, piece)
    loop(1, units - 1, lambda u: give(u + 1, u * unit, unit))
    for c, start in ends[2:]:
        give(c, start, piece)
    @pl.when(odd)
    def _():
        to_two.start()

    @pl.when(jnp.logical_not(odd))
    def _():
        to_one.start()

    loop(0, units, hold)

    def search(start, size, sections):
        block_c = cand[at(start, size), :]
        wide = block_c.astype(F32)
        half_square = 0.5 * jnp.sum(wide * wide, axis=1, keepdims=True)
        for s in sections:
            inner = lax.dot_general(block_c, pts[s], NT, preferred_element_type=F32)
            value = (half_square - inner).reshape(size // 8, 8, rows)
            mins[s] = jnp.minimum(mins[s], jnp.min(value, axis=0))

    def arrived(u, sections):
        chunk_copy(u + 1, u * unit, unit).wait_recv()
        search(u * unit, unit, sections)

    for c, start in ends[:2]:
        chunk_copy(c, start, piece).wait_recv()
    search(0, unit, (0,))
    loop(1, units // 2, lambda u: arrived(u, (0,)))
    to_one.wait_recv()

    @pl.when(odd)
    def _():
        handed.start()

    loop(0, units // 2, lambda u: search(u * unit, unit, (1,)))
    loop(units // 2, units - 2, lambda u: arrived(u, (0, 1)))
    to_two.wait_recv()
    loop(0, units - 2, lambda u: search(u * unit, unit, (2,)))
    arrived(units - 2, range(CYCLE + 1))
    for c, start in ends[2:]:
        chunk_copy(c, start, piece).wait_recv()
        search(start, piece, range(CYCLE + 1))

    back = []
    for s in range(CYCLE + 1):
        for way in range(2):
            if s == 0 and way == 0:
                continue
            back.append(pltpu.make_async_remote_copy(
                src_ref=mins.at[s], dst_ref=got.at[way, s],
                send_sem=min_send.at[way, s], recv_sem=min_recv.at[way, s],
                device_id=(lax.rem(me + s, n), other if way else side), device_id_type=MESH))
    for copy in back:
        copy.start()

    def gone(c, start, size):
        chunk_copy(c, start, size).wait_send()
        sent_out(c, start, size).wait()

    for c, start in ends:
        gone(c, start, piece)
    loop(1, units - 1, lambda u: gone(u + 1, u * unit, unit))
    loop(0, units, lambda u: kept_out(u).wait())
    to_one.wait_send()

    @pl.when(odd)
    def _():
        to_two.wait_send()
        handed.wait_send()

    for copy in back:
        copy.wait()
    best = mins[0]
    for s in range(CYCLE + 1):
        for way in range(2):
            if s or way:
                best = jnp.minimum(best, got[way, s])
    least = jnp.min(best, axis=0, keepdims=True)
    near_ref[...] = (squares[0:1, :] + 2.0 * least) / (2 * half)


def shards(points, owner, member, centroids):
    n = lax.axis_size("blk")
    rows, half = points.shape
    lists = centroids.shape[0]
    slots = 2 * rows // n
    units = 8
    chunks = units + 2
    total = n * slots
    anywhere, vmem = pl.BlockSpec(memory_space=pl.ANY), pl.BlockSpec(memory_space=pltpu.VMEM)
    dma = pltpu.SemaphoreType.DMA
    new, near = pl.pallas_call(
        functools.partial(kernel, n, slots, units),
        out_shape=(
            jax.ShapeDtypeStruct(centroids.shape, BF16),
            jax.ShapeDtypeStruct((1, rows), F32),
        ),
        in_specs=[vmem, vmem, anywhere, anywhere],
        out_specs=(anywhere, vmem),
        scratch_shapes=[
            pltpu.VMEM((CYCLE + 1, rows, 2 * half), BF16),
            pltpu.VMEM((lists, half), BF16),
            pltpu.VMEM((lists // 2, 2 * half), BF16),
            pltpu.VMEM((total, half), BF16),
            pltpu.VMEM((total, half), BF16),
            pltpu.VMEM((n, 8, LANES), I32),
            pltpu.VMEM((n, 8, LANES), I32),
            pltpu.VMEM((8, total), I32),
            pltpu.VMEM((8, rows), I32),
            pltpu.VMEM((CYCLE + 1, 8, rows), F32),
            pltpu.VMEM((2, CYCLE + 1, 8, rows), F32),
            pltpu.VMEM((8, rows), F32),
            dma((2,)), dma((n,)), dma((n,)), dma((n,)), dma((n,)), dma, dma,
            dma((CYCLE + 1,)), dma((CYCLE,)), dma((chunks,)), dma((chunks,)), dma((2, chunks)),
            dma((2, CYCLE + 1)), dma((2, CYCLE + 1)),
        ],
        compiler_params=pltpu.CompilerParams(
            collective_id=0, has_side_effects=True, vmem_limit_bytes=56 * 1024 * 1024),
    )(owner.reshape(1, rows), member.reshape(1, rows), points, centroids)
    return new, near.reshape(rows)


def solution(mesh):
    in_specs = (P("blk", "dim"), P("blk", None), P("blk"), P("blk", "dim"))
    out_specs = (P("blk", "dim"), P("blk"))
    return jax.shard_map(shards, mesh=mesh, in_specs=in_specs, out_specs=out_specs, check_vma=False)
```
